32 devices in a mesh: grp: 2 (over y), ha: 4 (over z), ta: 2 (over x), cam: 2 (over core).
Axes of the slice: x: 2, y: 2, z: 4, core: 2. Of those that a mesh axis runs over, the one named last changes fastest.
Arguments:
- video: bfloat16 [4, 8, 32, 48, 128], P(('grp', 'cam'), 'ta', 'ha'), parts along dimension 0, may hold values from -6 to 6
- norm1_gain: float32 [128], replicated, may hold values from 0.1 to 1.9
- norm1_shift: float32 [128], replicated, may hold values from -3 to 3
- conv1_weight: bfloat16 [3, 3, 3, 128, 128], replicated, may hold values from -0.109375 to 0.109375
- conv1_bias: float32 [128], replicated, may hold values from -3 to 3
- norm2_gain: float32 [128], replicated, may hold values from 0.1 to 1.9
- norm2_shift: float32 [128], replicated, may hold values from -3 to 3
- conv2_weight: bfloat16 [3, 3, 3, 128, 128], replicated, may hold values from -0.109375 to 0.109375
- conv2_bias: float32 [128], replicated, may hold values from -3 to 3
Outputs:
- encoded: bfloat16 [4, 8, 32, 48, 128], P(('grp', 'cam'), 'ta', 'ha'), parts along dimension 0
The draws below stay inside these ranges and needn't reach their ends.
There are 2 independent parts, one for each index of `grp`. The reference program is written for one: setup_inputs(seed, part) draws one part's arguments, and reference() takes and returns one part's arrays. A program takes and returns all parts, laid end to end along the dimension named above; an argument that names none is the same for every part. Nothing has to cross between parts.
All inputs are finite; a program needn't handle non-finite values.
Results may differ from the reference program's by a relative error of at most 0.0039.
Values may be sent and summed in bfloat16 or wider, within the bound.
A program may use at most 128 MiB of HBM per device.

```python
import jax
import jax.numpy as jnp
from jax import lax

C = 128
WID = 48
CAMS = 2
FRAMES = 8
HEIGHT = 32


def steps_of(own_key, extent, pieces, smallest, largest):
    level, own = 1.0, jax.random.fold_in(own_key, 6)
    for dim, shards_of in pieces:
        steps = jnp.exp(jax.random.uniform(jax.random.fold_in(own, dim), (shards_of,), jnp.float32, smallest / len(pieces), largest / len(pieces)))
        level = level * jnp.repeat(steps, extent[dim] // shards_of).reshape([-1 if axis == dim else 1 for axis in range(len(extent))])
    return level


def noise(stream_key, dims, scale, reach, pieces=(), dtype=jnp.bfloat16):
    level = steps_of(stream_key, dims, pieces, -0.22, 0.18) if pieces else 1.0
    drawn = jax.random.normal(stream_key, dims, jnp.float32) * scale * level
    return jnp.minimum(jnp.maximum(drawn, -reach), reach).astype(dtype)


def setup_inputs(seed: int = 0, part: int = 0) -> dict:
    seeds = jax.random.split(jax.random.key(seed), 10)
    part_keys = jax.random.split(jax.random.fold_in(seeds[9], part), 10)
    return {
        "video": noise(part_keys[0], (CAMS, FRAMES, HEIGHT, WID, C), 1.0, 6.0, ((0, 2), (1, 2), (2, 4))),
        "norm1_gain": jnp.clip(1.0 + 0.18 * jax.random.normal(seeds[1], (C,), jnp.float32), 0.1, 1.9),
        "norm1_shift": noise(seeds[2], (C,), 0.5, 3.0, (), jnp.float32),
        "conv1_weight": noise(seeds[3], (3, 3, 3, C, C), (27 * C) ** -0.5, 0.109375),
        "conv1_bias": noise(seeds[4], (C,), 0.5, 3.0, (), jnp.float32),
        "norm2_gain": jnp.clip(1.0 + 0.18 * jax.random.normal(seeds[5], (C,), jnp.float32), 0.1, 1.9),
        "norm2_shift": noise(seeds[6], (C,), 0.5, 3.0, (), jnp.float32),
        "conv2_weight": noise(seeds[7], (3, 3, 3, C, C), (27 * C) ** -0.5, 0.109375),
        "conv2_bias": noise(seeds[8], (C,), 0.5, 3.0, (), jnp.float32),
    }


def activate(values, gain, shift):
    middle = lax.optimization_barrier(jnp.mean(values, axis=-1, keepdims=True))
    centred = values - middle
    spread = lax.optimization_barrier(jnp.mean(centred * centred, axis=-1, keepdims=True))
    normed = centred * lax.rsqrt(spread + 1e-06) * gain.astype(jnp.float32) + shift.astype(jnp.float32)
    return jax.nn.silu(normed)

def convolve(layer_input, weight, bias):
    leading = layer_input[:, :1]
    padded = jnp.concatenate([leading, leading, layer_input], axis=1)
    padded = jnp.pad(padded, ((0, 0), (0, 0), (1, 1), (1, 1), (0, 0)))
    result = lax.conv_general_dilated(padded.astype(jnp.float32), weight.astype(jnp.float32), (1, 1, 1), 'VALID', dimension_numbers=('NDHWC', 'DHWIO', 'NDHWC'), precision=lax.Precision.HIGHEST)
    return result + bias.astype(jnp.float32)

def reference(video, norm1_gain, norm1_shift, conv1_weight, conv1_bias, norm2_gain, norm2_shift, conv2_weight, conv2_bias):
    inputs = video.astype(jnp.float32)
    first_input = activate(inputs, norm1_gain, norm1_shift).astype(jnp.bfloat16)
    first_out = convolve(first_input, conv1_weight, conv1_bias)
    second_input = activate(first_out, norm2_gain, norm2_shift).astype(jnp.bfloat16)
    second_out = convolve(second_input, conv2_weight, conv2_bias)
    return (inputs + second_out).astype(jnp.bfloat16)
```

```python
import functools

import jax
import jax.numpy as jnp
from jax import lax
from jax.experimental import pallas as pl
from jax.experimental.pallas import tpu as pltpu
from jax.sharding import PartitionSpec as P

MESH = pl.DeviceIdType.MESH
F32 = jnp.float32
BF16 = jnp.bfloat16


def activate(values, gain, shift):
    middle = jnp.mean(values, axis=-1, keepdims=True)
    centred = values - middle
    spread = jnp.mean(centred * centred, axis=-1, keepdims=True)
    normed = centred * lax.rsqrt(spread + 1e-06) * gain + shift
    half = 0.5 * normed
    return half + half * jnp.tanh(half)


def spread_columns(cells, width):
    total, channels = cells.shape
    column = lax.rem(lax.broadcasted_iota(jnp.int32, cells.shape, 0), width)
    left = jnp.where(column == 0, 0.0, pltpu.roll(cells, 1, 0))
    right = jnp.where(column == width - 1, 0.0, pltpu.roll(cells, total - 1, 0))
    wide = jnp.concatenate([left.astype(BF16), cells.astype(BF16), right.astype(BF16)], axis=-1)
    return wide.reshape(total // width, width, 3 * channels)


def kernel(
    video, g1, s1, w1, b1, g2, s2, w2, b2,
    out,
    vid, x1, x2, wb1, wb2, mid, obuf,
    vx, vtop, vbot, sx, stop, sbot,
    vsem, wsem, osem, send_v, recv_v, send_s, recv_s,
):
    frames, rows, width, channels = video.shape
    last = rows - 1
    ta, tn = lax.axis_index("ta"), lax.axis_size("ta")
    ha, hn = lax.axis_index("ha"), lax.axis_size("ha")
    has_prev, has_next = ta > 0, ta < tn - 1
    has_up, has_down = ha > 0, ha < hn - 1
    nxt, prv = {"ta": lax.rem(ta + 1, tn)}, {"ta": lax.rem(ta + tn - 1, tn)}
    up, down = {"ha": lax.rem(ha + hn - 1, hn)}, {"ha": lax.rem(ha + 1, hn)}

    barrier = pltpu.get_barrier_semaphore()
    for cond, dev in ((has_next, nxt), (has_prev, prv), (has_up, up), (has_down, down)):
        @pl.when(cond)
        def _():
            pl.semaphore_signal(barrier, inc=1, device_id=dev, device_id_type=MESH)

    vcopy = pltpu.make_async_copy(video, vid, vsem)
    vcopy.start()
    wcopies = []
    for i, (w, wb) in enumerate(((w1, wb1), (w2, wb2))):
        for o in range(2):
            copy = pltpu.make_async_copy(
                w, wb.at[o : o + 3, :, o * channels : (o + 1) * channels], wsem.at[i, o]
            )
            copy.start()
            wcopies.append(copy)
        wb[3, :, 0:channels] = jnp.zeros((wb.shape[1], channels), BF16)
        wb[0, :, channels : 2 * channels] = jnp.zeros((wb.shape[1], channels), BF16)

    amount = (
        has_next.astype(jnp.int32) + has_prev.astype(jnp.int32)
        + has_up.astype(jnp.int32) + has_down.astype(jnp.int32)
    )
    pl.semaphore_wait(barrier, amount)

    def remote(src, dst, sems, k, dev):
        return pltpu.make_async_remote_copy(
            src_ref=src, dst_ref=dst, send_sem=sems[0].at[k], recv_sem=sems[1].at[k],
            device_id=dev, device_id_type=MESH,
        )

    def plan(src, halo, top, bot, sems):
        tail = slice(frames - 2, frames)
        x = [
            remote(src.at[tail, 0], halo.at[:, 0], sems, 0, nxt),
            remote(src.at[tail, last], halo.at[:, last], sems, 1, nxt),
            remote(src.at[tail, 1:last], halo.at[:, 1:last], sems, 2, nxt),
        ]
        forward_up = remote(halo.at[:, 0], bot.at[0:2], sems, 3, up)
        forward_down = remote(halo.at[:, last], top.at[0:2], sems, 4, down)
        late = [
            remote(src.at[tail, 0], bot.at[4:6], sems, 5, up),
            remote(src.at[tail, last], top.at[4:6], sems, 6, down),
        ]
        early = [
            remote(src.at[0:2, 0], bot.at[2:4], sems, 7, up),
            remote(src.at[0:2, last], top.at[2:4], sems, 8, down),
        ]
        return x, (forward_up, forward_down), late, early

    vplan = plan(video, vx, vtop, vbot, (send_v, recv_v))
    splan = plan(mid, sx, stop, sbot, (send_s, recv_s))

    def start_x(p):
        @pl.when(has_next)
        def _():
            for c in p[0]:
                c.start()

    def start_z(pair):
        @pl.when(has_up)
        def _():
            pair[0].start()

        @pl.when(has_down)
        def _():
            pair[1].start()

    def wait_z(pair):
        @pl.when(has_down)
        def _():
            pair[0].wait_recv()

        @pl.when(has_up)
        def _():
            pair[1].wait_recv()

    def forward(p):
        @pl.when(has_prev)
        def _():
            for c in p[0][0:2]:
                c.wait_recv()
            start_z(p[1])

    def wait_forward(p):
        p[0][2].wait_recv()
        wait_z(p[1])

    def finish_sends(p):
        @pl.when(has_next)
        def _():
            for c in p[0]:
                c.wait_send()
        for pair in (p[2], p[3]):
            @pl.when(has_up)
            def _():
                pair[0].wait_send()

            @pl.when(has_down)
            def _():
                pair[1].wait_send()

        @pl.when(has_prev & has_up)
        def _():
            p[1][0].wait_send()

        @pl.when(has_prev & has_down)
        def _():
            p[1][1].wait_send()

    start_z(vplan[2])
    start_x(vplan)
    start_z(vplan[3])

    gain1, shift1 = g1[...].reshape(1, channels), s1[...].reshape(1, channels)
    gain2, shift2 = g2[...].reshape(1, channels), s2[...].reshape(1, channels)
    bias1, bias2 = b1[...].reshape(1, channels), b2[...].reshape(1, channels)
    zero_row = jnp.zeros((width, 3 * channels), BF16)

    def first(cells):
        flat = cells.astype(F32).reshape(-1, channels)
        return spread_columns(activate(flat, gain1, shift1), width)

    def plain(cells):
        return spread_columns(cells.astype(F32).reshape(-1, channels), width)

    def edges(x, top, bot, exts, make):
        for cond, halo, row in ((has_up, top, 0), (has_down, bot, rows + 1)):
            @pl.when(cond)
            def _():
                made = make(halo[exts[0] : exts[-1] + 1])
                for k, e in enumerate(exts):
                    x[e, row] = made[k]

            @pl.when(jnp.logical_not(cond))
            def _():
                for e in exts:
                    x[e, row] = zero_row

    def lead(x, p, halo, top, bot, make):
        @pl.when(has_prev)
        def _():
            wait_forward(p)
            for e in range(2):
                x[e, 1 : rows + 1] = make(halo[e])
            edges(x, top, bot, (0, 1), make)

        @pl.when(jnp.logical_not(has_prev))
        def _():
            for e in range(2):
                x[e] = x[2]

    def conv(x, wb, group, row, count):
        combos = [(r, di) for r in range(4) for di in range(3)]
        depth = 3 * channels
        total = None
        for c in range(0, 12, 2):
            cells = jnp.concatenate(
                [
                    x[2 * group + r, row + di : row + di + count].reshape(count * width, depth)
                    for r, di in combos[c : c + 2]
                ],
                axis=-1,
            )
            weight = jnp.concatenate(
                [wb[r, di * depth : (di + 1) * depth, :] for r, di in combos[c : c + 2]], axis=0
            )
            product = jnp.dot(cells, weight, preferred_element_type=F32)
            total = product if total is None else total + product
        return total

    def conv1(group, row, count):
        summed = conv(x1, wb1, group, row, count)
        for o in range(2):
            part = summed[:, o * channels : (o + 1) * channels] + bias1
            part = activate(part, gain2, shift2)
            frame = 2 * group + o
            mid[frame, row : row + count] = part.astype(BF16).reshape(count, width, channels)
            x2[frame + 2, row + 1 : row + 1 + count] = spread_columns(part, width)

    def conv2(group, row, count):
        summed = conv(x2, wb2, group, row, count)
        for o in range(2):
            part = summed[:, o * channels : (o + 1) * channels] + bias2
            frame = 2 * group + o
            base = vid[frame, row : row + count].astype(F32).reshape(count * width, channels)
            obuf[frame, row : row + count] = (base + part).astype(BF16).reshape(count, width, channels)

    vcopy.wait()
    for f in range(frames):
        x1[f + 2, 1 : rows + 1] = first(vid[f])
    wait_z(vplan[2])
    wait_z(vplan[3])
    edges(x1, vtop, vbot, (2, 3, 4, 5), first)
    forward(vplan)
    wcopies[0].wait()
    wcopies[1].wait()
    conv1(1, 0, rows)
    start_z(splan[2])
    start_x(splan)
    lead(x1, vplan, vx, vtop, vbot, first)
    conv1(0, 0, rows)
    start_z(splan[3])
    wcopies[2].wait()
    wcopies[3].wait()
    forward(splan)
    wait_z(splan[2])
    edges(x2, stop, sbot, (4, 5), plain)
    conv2(1, 1, rows - 2)
    wait_z(splan[3])
    edges(x2, stop, sbot, (2, 3), plain)
    conv2(1, 0, 1)
    conv2(1, last, 1)
    ocopies = [
        pltpu.make_async_copy(obuf.at[2 * g : 2 * g + 2], out.at[2 * g : 2 * g + 2], osem.at[g])
        for g in range(2)
    ]
    ocopies[1].start()
    lead(x2, splan, sx, stop, sbot, plain)
    conv2(0, 0, rows)
    ocopies[0].start()
    finish_sends(vplan)
    finish_sends(splan)
    ocopies[1].wait()
    ocopies[0].wait()


def body(video, g1, s1, w1, b1, g2, s2, w2, b2):
    own = video[0]
    frames, rows, width, channels = own.shape
    flat = (3, 9 * channels, channels)
    hbm = pl.BlockSpec(memory_space=pl.ANY)
    vmem = pl.BlockSpec(memory_space=pltpu.VMEM)
    ext = (frames + 2, rows + 2, width, 3 * channels)
    halo = [
        pltpu.VMEM((2, rows, width, channels), BF16),
        pltpu.VMEM((frames + 2, width, channels), BF16),
        pltpu.VMEM((frames + 2, width, channels), BF16),
    ]
    big = pltpu.VMEM((4, 9 * channels, 2 * channels), BF16)
    own_scratch = pltpu.VMEM(own.shape, BF16)
    dma = pltpu.SemaphoreType.DMA
    result = pl.pallas_call(
        kernel,
        out_shape=jax.ShapeDtypeStruct(own.shape, BF16),
        in_specs=[hbm, vmem, vmem, hbm, vmem, vmem, vmem, hbm, vmem],
        out_specs=hbm,
        scratch_shapes=[
            own_scratch,
            pltpu.VMEM(ext, BF16), pltpu.VMEM(ext, BF16),
            big, big,
            own_scratch, own_scratch,
            *halo, *halo,
            dma(()), dma((2, 2)), dma((2,)),
            dma((9,)), dma((9,)), dma((9,)), dma((9,)),
        ],
        compiler_params=pltpu.CompilerParams(
            collective_id=0, has_side_effects=True, vmem_limit_bytes=56 * 2**20
        ),
        cost_estimate=pl.CostEstimate(
            flops=4 * own.size * 27 * channels,
            bytes_accessed=4 * own.size + 8 * w1.size,
            transcendentals=2 * own.size,
        ),
    )(own, g1, s1, w1.reshape(flat), b1, g2, s2, w2.reshape(flat), b2)
    return result[None]


def solution(mesh):
    placed = (P(("grp", "cam"), "ta", "ha", None, None), P(), P(), P(), P(), P(), P(), P(), P())
    return jax.shard_map(
        body,
        mesh=mesh,
        in_specs=placed,
        out_specs=P(("grp", "cam"), "ta", "ha", None, None),
        check_vma=False,
    )
```

```python
import functools

import jax
import jax.numpy as jnp
from jax import lax
from jax.experimental import pallas as pl
from jax.experimental.pallas import tpu as pltpu
from jax.sharding import PartitionSpec as P

MESH = pl.DeviceIdType.MESH
F32 = jnp.float32
BF16 = jnp.bfloat16


def activate(values, gain, shift):
    middle = jnp.mean(values, axis=-1, keepdims=True)
    centred = values - middle
    spread = jnp.mean(centred * centred, axis=-1, keepdims=True)
    normed = centred * lax.rsqrt(spread + 1e-06) * gain + shift
    half = 0.5 * normed
    return half + half * jnp.tanh(half)


def spread_columns(cells, width):
    total, channels = cells.shape
    column = lax.rem(lax.broadcasted_iota(jnp.int32, cells.shape, 0), width)
    left = jnp.where(column == 0, 0.0, pltpu.roll(cells, 1, 0))
    right = jnp.where(column == width - 1, 0.0, pltpu.roll(cells, total - 1, 0))
    wide = jnp.concatenate([left.astype(BF16), cells.astype(BF16), right.astype(BF16)], axis=-1)
    return wide.reshape(total // width, width, 3 * channels)


def kernel(
    video, hg1, hs1, w1, hb1, hg2, hs2, w2, hb2,
    out,
    g1, s1, b1, g2, s2, b2,
    vid, x1, x2, wb1, wb2, mid,
    vx, vtop, vbot, sx, stop, sbot,
    vsem, psem, wsem, send_v, recv_v, send_s, recv_s,
):
    frames, rows, width, channels = video.shape
    last = rows - 1
    ta, tn = lax.axis_index("ta"), lax.axis_size("ta")
    ha, hn = lax.axis_index("ha"), lax.axis_size("ha")
    has_prev, has_next = ta > 0, ta < tn - 1
    has_up, has_down = ha > 0, ha < hn - 1
    nxt, prv = {"ta": lax.rem(ta + 1, tn)}, {"ta": lax.rem(ta + tn - 1, tn)}
    up, down = {"ha": lax.rem(ha + hn - 1, hn)}, {"ha": lax.rem(ha + 1, hn)}

    barrier = pltpu.get_barrier_semaphore()
    for cond, dev in ((has_next, nxt), (has_prev, prv), (has_up, up), (has_down, down)):
        @pl.when(cond)
        def _():
            pl.semaphore_signal(barrier, inc=1, device_id=dev, device_id_type=MESH)

    vcopy = pltpu.make_async_copy(video, vid, vsem)
    vcopy.start()
    params = ((hg1, g1), (hs1, s1), (hb1, b1), (hg2, g2), (hs2, s2), (hb2, b2))
    pcopies = [pltpu.make_async_copy(h, v, psem.at[i]) for i, (h, v) in enumerate(params)]
    for copy in pcopies:
        copy.start()
    wcopies = []
    for i, (w, wb) in enumerate(((w1, wb1), (w2, wb2))):
        for o in range(2):
            copy = pltpu.make_async_copy(
                w, wb.at[o : o + 3, :, o * channels : (o + 1) * channels], wsem.at[i, o]
            )
            copy.start()
            wcopies.append(copy)
        wb[3, :, 0:channels] = jnp.zeros((wb.shape[1], channels), BF16)
        wb[0, :, channels : 2 * channels] = jnp.zeros((wb.shape[1], channels), BF16)

    amount = (
        has_next.astype(jnp.int32) + has_prev.astype(jnp.int32)
        + has_up.astype(jnp.int32) + has_down.astype(jnp.int32)
    )
    pl.semaphore_wait(barrier, amount)

    def remote(src, dst, sems, k, dev):
        return pltpu.make_async_remote_copy(
            src_ref=src, dst_ref=dst, send_sem=sems[0].at[k], recv_sem=sems[1].at[k],
            device_id=dev, device_id_type=MESH,
        )

    def plan(src, halo, top, bot, sems):
        tail = slice(frames - 2, frames)
        x = [
            remote(src.at[tail, 0], halo.at[:, 0], sems, 0, nxt),
            remote(src.at[tail, last], halo.at[:, last], sems, 1, nxt),
            remote(src.at[tail, 1:last], halo.at[:, 1:last], sems, 2, nxt),
        ]
        forward_up = remote(halo.at[:, 0], bot.at[0:2], sems, 3, up)
        forward_down = remote(halo.at[:, last], top.at[0:2], sems, 4, down)
        late = [
            remote(src.at[tail, 0], bot.at[4:6], sems, 5, up),
            remote(src.at[tail, last], top.at[4:6], sems, 6, down),
        ]
        early = [
            remote(src.at[0:2, 0], bot.at[2:4], sems, 7, up),
            remote(src.at[0:2, last], top.at[2:4], sems, 8, down),
        ]
        return x, (forward_up, forward_down), late, early

    vplan = plan(video, vx, vtop, vbot, (send_v, recv_v))
    splan = plan(mid, sx, stop, sbot, (send_s, recv_s))

    def start_x(p):
        @pl.when(has_next)
        def _():
            for c in p[0]:
                c.start()

    def start_z(pair):
        @pl.when(has_up)
        def _():
            pair[0].start()

        @pl.when(has_down)
        def _():
            pair[1].start()

    def wait_z(pair):
        @pl.when(has_down)
        def _():
            pair[0].wait_recv()

        @pl.when(has_up)
        def _():
            pair[1].wait_recv()

    def forward(p):
        @pl.when(has_prev)
        def _():
            for c in p[0][0:2]:
                c.wait_recv()
            start_z(p[1])

    def wait_forward(p):
        p[0][2].wait_recv()
        wait_z(p[1])

    def finish_sends(p):
        @pl.when(has_next)
        def _():
            for c in p[0]:
                c.wait_send()
        for pair in (p[2], p[3]):
            @pl.when(has_up)
            def _():
                pair[0].wait_send()

            @pl.when(has_down)
            def _():
                pair[1].wait_send()

        @pl.when(has_prev & has_up)
        def _():
            p[1][0].wait_send()

        @pl.when(has_prev & has_down)
        def _():
            p[1][1].wait_send()

    start_z(vplan[2])
    start_x(vplan)
    start_z(vplan[3])

    for copy in pcopies:
        copy.wait()
    gain1, shift1 = g1[...].reshape(1, channels), s1[...].reshape(1, channels)
    gain2, shift2 = g2[...].reshape(1, channels), s2[...].reshape(1, channels)
    bias1, bias2 = b1[...].reshape(1, channels), b2[...].reshape(1, channels)
    zero_row = jnp.zeros((width, 3 * channels), BF16)

    def first(cells):
        flat = cells.astype(F32).reshape(-1, channels)
        return spread_columns(activate(flat, gain1, shift1), width)

    def plain(cells):
        return spread_columns(cells.astype(F32).reshape(-1, channels), width)

    def edges(x, top, bot, exts, make):
        for cond, halo, row in ((has_up, top, 0), (has_down, bot, rows + 1)):
            @pl.when(cond)
            def _():
                made = make(halo[exts[0] : exts[-1] + 1])
                for k, e in enumerate(exts):
                    x[e, row] = made[k]

            @pl.when(jnp.logical_not(cond))
            def _():
                for e in exts:
                    x[e, row] = zero_row

    def lead(x, p, halo, top, bot, make):
        @pl.when(has_prev)
        def _():
            wait_forward(p)
            for e in range(2):
                x[e, 1 : rows + 1] = make(halo[e])
            edges(x, top, bot, (0, 1), make)

        @pl.when(jnp.logical_not(has_prev))
        def _():
            for e in range(2):
                x[e] = x[2]

    def conv(x, wb, group, row, count):
        combos = [(r, di) for r in range(4) for di in range(3)]
        depth = 3 * channels
        total = None
        for c in range(0, 12, 2):
            cells = jnp.concatenate(
                [
                    x[2 * group + r, row + di : row + di + count].reshape(count * width, depth)
                    for r, di in combos[c : c + 2]
                ],
                axis=-1,
            )
            weight = jnp.concatenate(
                [wb[r, di * depth : (di + 1) * depth, :] for r, di in combos[c : c + 2]], axis=0
            )
            product = jnp.dot(cells, weight, preferred_element_type=F32)
            total = product if total is None else total + product
        return total

    def conv1(group, row, count):
        summed = conv(x1, wb1, group, row, count)
        for o in range(2):
            part = summed[:, o * channels : (o + 1) * channels] + bias1
            part = activate(part, gain2, shift2)
            frame = 2 * group + o
            mid[frame, row : row + count] = part.astype(BF16).reshape(count, width, channels)
            x2[frame + 2, row + 1 : row + 1 + count] = spread_columns(part, width)

    def conv2(group, row, count):
        summed = conv(x2, wb2, group, row, count)
        for o in range(2):
            part = summed[:, o * channels : (o + 1) * channels] + bias2
            frame = 2 * group + o
            base = vid[frame, row : row + count].astype(F32).reshape(count * width, channels)
            out[frame, row : row + count] = (base + part).astype(BF16).reshape(count, width, channels)

    vcopy.wait()
    for f in range(frames):
        x1[f + 2, 1 : rows + 1] = first(vid[f])
    wait_z(vplan[2])
    wait_z(vplan[3])
    edges(x1, vtop, vbot, (2, 3, 4, 5), first)
    forward(vplan)
    wcopies[0].wait()
    wcopies[1].wait()
    conv1(1, 0, rows)
    start_z(splan[2])
    start_x(splan)
    lead(x1, vplan, vx, vtop, vbot, first)
    conv1(0, 0, rows)
    start_z(splan[3])
    wcopies[2].wait()
    wcopies[3].wait()
    forward(splan)
    wait_z(splan[2])
    edges(x2, stop, sbot, (4, 5), plain)
    conv2(1, 1, rows - 2)
    wait_z(splan[3])
    edges(x2, stop, sbot, (2, 3), plain)
    conv2(1, 0, 1)
    conv2(1, last, 1)
    lead(x2, splan, sx, stop, sbot, plain)
    conv2(0, 0, rows)
    finish_sends(vplan)
    finish_sends(splan)


def body(video, g1, s1, w1, b1, g2, s2, w2, b2):
    own = video[0]
    in_hbm = functools.partial(pltpu.with_memory_space_constraint, memory_space=pltpu.HBM)
    frames, rows, width, channels = own.shape
    flat = (3, 9 * channels, channels)
    hbm = pl.BlockSpec(memory_space=pltpu.HBM)
    vmem = pl.BlockSpec(memory_space=pltpu.VMEM)
    ext = (frames + 2, rows + 2, width, 3 * channels)
    halo = [
        pltpu.VMEM((2, rows, width, channels), BF16),
        pltpu.VMEM((frames + 2, width, channels), BF16),
        pltpu.VMEM((frames + 2, width, channels), BF16),
    ]
    big = pltpu.VMEM((4, 9 * channels, 2 * channels), BF16)
    own_scratch = pltpu.VMEM(own.shape, BF16)
    dma = pltpu.SemaphoreType.DMA
    result = pl.pallas_call(
        kernel,
        out_shape=pltpu.VMEM(own.shape, BF16),
        in_specs=[hbm] * 9,
        out_specs=vmem,
        scratch_shapes=[
            *[pltpu.VMEM((channels,), F32)] * 6,
            own_scratch,
            pltpu.VMEM(ext, BF16), pltpu.VMEM(ext, BF16),
            big, big,
            own_scratch,
            *halo, *halo,
            dma(()), dma((6,)), dma((2, 2)),
            dma((9,)), dma((9,)), dma((9,)), dma((9,)),
        ],
        compiler_params=pltpu.CompilerParams(
            collective_id=0, has_side_effects=True, vmem_limit_bytes=40 * 2**20
        ),
        cost_estimate=pl.CostEstimate(
            flops=4 * own.size * 27 * channels,
            bytes_accessed=4 * own.size + 8 * w1.size,
            transcendentals=2 * own.size,
        ),
    )(*[in_hbm(a) for a in (own, g1, s1, w1.reshape(flat), b1, g2, s2, w2.reshape(flat), b2)])
    return result[None]


def solution(mesh):
    placed = (P(("grp", "cam"), "ta", "ha", None, None), P(), P(), P(), P(), P(), P(), P(), P())
    return jax.shard_map(
        body,
        mesh=mesh,
        in_specs=placed,
        out_specs=P(("grp", "cam"), "ta", "ha", None, None),
        check_vma=False,
    )
```

```python
import functools

import jax
import jax.numpy as jnp
from jax import lax
from jax.experimental import pallas as pl
from jax.experimental.pallas import tpu as pltpu
from jax.sharding import PartitionSpec as P

MESH = pl.DeviceIdType.MESH
F32 = jnp.float32
BF16 = jnp.bfloat16


def activate(values, gain, shift):
    middle = jnp.mean(values, axis=-1, keepdims=True)
    centred = values - middle
    spread = jnp.mean(centred * centred, axis=-1, keepdims=True)
    normed = centred * lax.rsqrt(spread + 1e-06) * gain + shift
    half = 0.5 * normed
    return half + half * jnp.tanh(half)


def spread_columns(cells, width):
    total, channels = cells.shape
    column = lax.rem(lax.broadcasted_iota(jnp.int32, cells.shape, 0), width)
    left = jnp.where(column == 0, 0.0, pltpu.roll(cells, 1, 0))
    right = jnp.where(column == width - 1, 0.0, pltpu.roll(cells, total - 1, 0))
    wide = jnp.concatenate([left.astype(BF16), cells.astype(BF16), right.astype(BF16)], axis=-1)
    return wide.reshape(total // width, width, 3 * channels)


def kernel(
    video, hg1, hs1, w1, hb1, hg2, hs2, w2, hb2,
    out,
    g1, s1, b1, g2, s2, b2,
    vid, x1, x2, wb1, wb2, mid, acc,
    vx, vtop, vbot, sx, stop, sbot,
    vsem, psem, wsem, send_v, recv_v, send_s, recv_s,
):
    frames, rows, width, channels = video.shape
    last = rows - 1
    ta, tn = lax.axis_index("ta"), lax.axis_size("ta")
    ha, hn = lax.axis_index("ha"), lax.axis_size("ha")
    has_prev, has_next = ta > 0, ta < tn - 1
    has_up, has_down = ha > 0, ha < hn - 1
    nxt, prv = {"ta": lax.rem(ta + 1, tn)}, {"ta": lax.rem(ta + tn - 1, tn)}
    up, down = {"ha": lax.rem(ha + hn - 1, hn)}, {"ha": lax.rem(ha + 1, hn)}

    barrier = pltpu.get_barrier_semaphore()
    for cond, dev in ((has_next, nxt), (has_prev, prv), (has_up, up), (has_down, down)):
        @pl.when(cond)
        def _():
            pl.semaphore_signal(barrier, inc=1, device_id=dev, device_id_type=MESH)

    vcopy = pltpu.make_async_copy(video, vid, vsem)
    vcopy.start()
    params = ((hg1, g1), (hs1, s1), (hb1, b1), (hg2, g2), (hs2, s2), (hb2, b2))
    pcopies = [pltpu.make_async_copy(h, v, psem.at[i]) for i, (h, v) in enumerate(params)]
    for copy in pcopies:
        copy.start()
    wcopies = []
    for i, (w, wb) in enumerate(((w1, wb1), (w2, wb2))):
        for o in range(2):
            copy = pltpu.make_async_copy(
                w, wb.at[o : o + 3, :, o * channels : (o + 1) * channels], wsem.at[i, o]
            )
            copy.start()
            wcopies.append(copy)
        wb[3, :, 0:channels] = jnp.zeros((wb.shape[1], channels), BF16)
        wb[0, :, channels : 2 * channels] = jnp.zeros((wb.shape[1], channels), BF16)

    amount = (
        has_next.astype(jnp.int32) + has_prev.astype(jnp.int32)
        + has_up.astype(jnp.int32) + has_down.astype(jnp.int32)
    )
    pl.semaphore_wait(barrier, amount)

    def remote(src, dst, sems, k, dev):
        return pltpu.make_async_remote_copy(
            src_ref=src, dst_ref=dst, send_sem=sems[0].at[k], recv_sem=sems[1].at[k],
            device_id=dev, device_id_type=MESH,
        )

    def plan(src, halo, top, bot, sems):
        tail = slice(frames - 2, frames)
        x = [
            remote(src.at[tail, 0], halo.at[:, 0], sems, 0, nxt),
            remote(src.at[tail, last], halo.at[:, last], sems, 1, nxt),
            remote(src.at[tail, 1:last], halo.at[:, 1:last], sems, 2, nxt),
        ]
        forward_up = remote(halo.at[:, 0], bot.at[0:2], sems, 3, up)
        forward_down = remote(halo.at[:, last], top.at[0:2], sems, 4, down)
        late = [
            remote(src.at[tail, 0], bot.at[4:6], sems, 5, up),
            remote(src.at[tail, last], top.at[4:6], sems, 6, down),
        ]
        early = [
            remote(src.at[0:2, 0], bot.at[2:4], sems, 7, up),
            remote(src.at[0:2, last], top.at[2:4], sems, 8, down),
        ]
        return x, (forward_up, forward_down), late, early

    vplan = plan(video, vx, vtop, vbot, (send_v, recv_v))
    splan = plan(mid, sx, stop, sbot, (send_s, recv_s))

    def start_x(p):
        @pl.when(has_next)
        def _():
            for c in p[0]:
                c.start()

    def start_z(pair):
        @pl.when(has_up)
        def _():
            pair[0].start()

        @pl.when(has_down)
        def _():
            pair[1].start()

    def wait_z(pair):
        @pl.when(has_down)
        def _():
            pair[0].wait_recv()

        @pl.when(has_up)
        def _():
            pair[1].wait_recv()

    def forward(p):
        @pl.when(has_prev)
        def _():
            for c in p[0][0:2]:
                c.wait_recv()
            start_z(p[1])

    def wait_forward(p):
        p[0][2].wait_recv()
        wait_z(p[1])

    def finish_sends(p):
        @pl.when(has_next)
        def _():
            for c in p[0]:
                c.wait_send()
        for pair in (p[2], p[3]):
            @pl.when(has_up)
            def _():
                pair[0].wait_send()

            @pl.when(has_down)
            def _():
                pair[1].wait_send()

        @pl.when(has_prev & has_up)
        def _():
            p[1][0].wait_send()

        @pl.when(has_prev & has_down)
        def _():
            p[1][1].wait_send()

    start_z(vplan[2])
    start_x(vplan)
    start_z(vplan[3])

    for copy in pcopies:
        copy.wait()
    gain1, shift1 = g1[...].reshape(1, channels), s1[...].reshape(1, channels)
    gain2, shift2 = g2[...].reshape(1, channels), s2[...].reshape(1, channels)
    bias1, bias2 = b1[...].reshape(1, channels), b2[...].reshape(1, channels)
    zero_row = jnp.zeros((width, 3 * channels), BF16)

    def first(cells):
        flat = cells.astype(F32).reshape(-1, channels)
        return spread_columns(activate(flat, gain1, shift1), width)

    def plain(cells):
        return spread_columns(cells.astype(F32).reshape(-1, channels), width)

    def edges(x, top, bot, exts, make):
        for cond, halo, row in ((has_up, top, 0), (has_down, bot, rows + 1)):
            @pl.when(cond)
            def _():
                made = make(halo[exts[0] : exts[-1] + 1])
                for k, e in enumerate(exts):
                    x[e, row] = made[k]

            @pl.when(jnp.logical_not(cond))
            def _():
                for e in exts:
                    x[e, row] = zero_row

    def lead(x, p, halo, top, bot, make):
        @pl.when(has_prev)
        def _():
            wait_forward(p)
            for e in range(2):
                x[e, 1 : rows + 1] = make(halo[e])
            edges(x, top, bot, (0, 1), make)

        @pl.when(jnp.logical_not(has_prev))
        def _():
            for e in range(2):
                x[e] = x[2]

    def conv(x, wb, group, pieces, steps):
        combos = [(r, di) for r in steps for di in range(3)]
        depth = 3 * channels
        total = None
        for c in range(0, len(combos), 2):
            cells = jnp.concatenate(
                [
                    jnp.concatenate(
                        [
                            x[2 * group + r, row + di : row + di + count].reshape(count * width, depth)
                            for row, count in pieces
                        ],
                        axis=0,
                    )
                    for r, di in combos[c : c + 2]
                ],
                axis=-1,
            )
            weight = jnp.concatenate(
                [wb[r, di * depth : (di + 1) * depth, :] for r, di in combos[c : c + 2]], axis=0
            )
            product = jnp.dot(cells, weight, preferred_element_type=F32)
            total = product if total is None else total + product
        return total

    def cut(block, pieces):
        start = 0
        for row, count in pieces:
            yield row, count, block[start : start + count]
            start += count

    def finish1(summed, group, pieces):
        for o in range(2):
            part = summed[:, o * channels : (o + 1) * channels] + bias1
            part = activate(part, gain2, shift2)
            frame = 2 * group + o
            narrow = part.astype(BF16).reshape(-1, width, channels)
            for row, count, block in cut(narrow, pieces):
                mid[frame, row : row + count] = block
            for row, count, block in cut(spread_columns(part, width), pieces):
                x2[frame + 2, row + 1 : row + 1 + count] = block

    def finish2(summed, group, pieces):
        for o in range(2):
            part = summed[:, o * channels : (o + 1) * channels] + bias2
            frame = 2 * group + o
            for row, count, block in cut(part.reshape(-1, width, channels), pieces):
                base = vid[frame, row : row + count].astype(F32)
                out[frame, row : row + count] = (base + block).astype(BF16)

    whole = [(0, rows)]
    inner = [(1, rows - 2)]
    outer = [(0, 1), (last, 1)]
    every = range(4)

    vcopy.wait()
    for f in range(frames):
        x1[f + 2, 1 : rows + 1] = first(vid[f])
    wcopies[0].wait()
    wcopies[1].wait()
    finish1(conv(x1, wb1, 1, inner, every), 1, inner)
    wait_z(vplan[2])
    wait_z(vplan[3])
    edges(x1, vtop, vbot, (2, 3, 4, 5), first)
    finish1(conv(x1, wb1, 1, outer, every), 1, outer)
    start_z(splan[2])
    start_x(splan)
    forward(vplan)
    acc[...] = conv(x1, wb1, 0, whole, (2, 3))
    lead(x1, vplan, vx, vtop, vbot, first)
    finish1(acc[...] + conv(x1, wb1, 0, whole, (0, 1)), 0, whole)
    start_z(splan[3])
    forward(splan)
    wcopies[2].wait()
    wcopies[3].wait()
    finish2(conv(x2, wb2, 1, inner, every), 1, inner)
    wait_z(splan[2])
    wait_z(splan[3])
    edges(x2, stop, sbot, (2, 3, 4, 5), plain)
    finish2(conv(x2, wb2, 1, outer, every), 1, outer)
    acc[...] = conv(x2, wb2, 0, whole, (2, 3))
    lead(x2, splan, sx, stop, sbot, plain)
    finish2(acc[...] + conv(x2, wb2, 0, whole, (0, 1)), 0, whole)
    finish_sends(vplan)
    finish_sends(splan)


def body(video, g1, s1, w1, b1, g2, s2, w2, b2):
    own = video[0]
    in_hbm = functools.partial(pltpu.with_memory_space_constraint, memory_space=pltpu.HBM)
    frames, rows, width, channels = own.shape
    flat = (3, 9 * channels, channels)
    hbm = pl.BlockSpec(memory_space=pltpu.HBM)
    vmem = pl.BlockSpec(memory_space=pltpu.VMEM)
    ext = (frames + 2, rows + 2, width, 3 * channels)
    halo = [
        pltpu.VMEM((2, rows, width, channels), BF16),
        pltpu.VMEM((frames + 2, width, channels), BF16),
        pltpu.VMEM((frames + 2, width, channels), BF16),
    ]
    big = pltpu.VMEM((4, 9 * channels, 2 * channels), BF16)
    own_scratch = pltpu.VMEM(own.shape, BF16)
    dma = pltpu.SemaphoreType.DMA
    result = pl.pallas_call(
        kernel,
        out_shape=pltpu.VMEM(own.shape, BF16),
        in_specs=[hbm] * 9,
        out_specs=vmem,
        scratch_shapes=[
            *[pltpu.VMEM((channels,), F32)] * 6,
            own_scratch,
            pltpu.VMEM(ext, BF16), pltpu.VMEM(ext, BF16),
            big, big,
            own_scratch,
            pltpu.VMEM((rows * width, 2 * channels), F32),
            *halo, *halo,
            dma(()), dma((6,)), dma((2, 2)),
            dma((9,)), dma((9,)), dma((9,)), dma((9,)),
        ],
        compiler_params=pltpu.CompilerParams(
            collective_id=0, has_side_effects=True, vmem_limit_bytes=40 * 2**20
        ),
        cost_estimate=pl.CostEstimate(
            flops=4 * own.size * 27 * channels,
            bytes_accessed=4 * own.size + 8 * w1.size,
            transcendentals=2 * own.size,
        ),
    )(*[in_hbm(a) for a in (own, g1, s1, w1.reshape(flat), b1, g2, s2, w2.reshape(flat), b2)])
    return result[None]


def solution(mesh):
    placed = (P(("grp", "cam"), "ta", "ha", None, None), P(), P(), P(), P(), P(), P(), P(), P())
    return jax.shard_map(
        body,
        mesh=mesh,
        in_specs=placed,
        out_specs=P(("grp", "cam"), "ta", "ha", None, None),
        check_vma=False,
    )
```

```python
import functools

import jax
import jax.numpy as jnp
from jax import lax
from jax.experimental import pallas as pl
from jax.experimental.pallas import tpu as pltpu
from jax.sharding import PartitionSpec as P

MESH = pl.DeviceIdType.MESH
F32 = jnp.float32
BF16 = jnp.bfloat16


def activate(values, gain, shift):
    middle = jnp.mean(values, axis=-1, keepdims=True)
    centred = values - middle
    spread = jnp.mean(centred * centred, axis=-1, keepdims=True)
    normed = centred * lax.rsqrt(spread + 1e-06) * gain + shift
    half = 0.5 * normed
    return half + half * jnp.tanh(half)


def spread_columns(cells, width):
    total, channels = cells.shape
    column = lax.rem(lax.broadcasted_iota(jnp.int32, cells.shape, 0), width)
    left = jnp.where(column == 0, 0.0, pltpu.roll(cells, 1, 0))
    right = jnp.where(column == width - 1, 0.0, pltpu.roll(cells, total - 1, 0))
    wide = jnp.concatenate([left.astype(BF16), cells.astype(BF16), right.astype(BF16)], axis=-1)
    return wide.reshape(total // width, width, 3 * channels)


def kernel(
    video, hg1, hs1, w1, hb1, hg2, hs2, w2, hb2,
    out,
    g1, s1, b1, g2, s2, b2,
    vid, x1, x2, wb1, wb2, mid, acc,
    vx, vtop, vbot, sx, stop, sbot,
    vsem, psem, wsem, send_v, recv_v, send_s, recv_s,
):
    frames, rows, width, channels = video.shape
    last = rows - 1
    ta, tn = lax.axis_index("ta"), lax.axis_size("ta")
    ha, hn = lax.axis_index("ha"), lax.axis_size("ha")
    has_prev, has_next = ta > 0, ta < tn - 1
    has_up, has_down = ha > 0, ha < hn - 1
    nxt, prv = {"ta": lax.rem(ta + 1, tn)}, {"ta": lax.rem(ta + tn - 1, tn)}
    up, down = {"ha": lax.rem(ha + hn - 1, hn)}, {"ha": lax.rem(ha + 1, hn)}

    barrier = pltpu.get_barrier_semaphore()
    for cond, dev in ((has_next, nxt), (has_prev, prv), (has_up, up), (has_down, down)):
        @pl.when(cond)
        def _():
            pl.semaphore_signal(barrier, inc=1, device_id=dev, device_id_type=MESH)

    vcopy = pltpu.make_async_copy(video, vid, vsem)
    vcopy.start()
    params = ((hg1, g1), (hs1, s1), (hb1, b1), (hg2, g2), (hs2, s2), (hb2, b2))
    pcopies = [pltpu.make_async_copy(h, v, psem.at[i]) for i, (h, v) in enumerate(params)]
    for copy in pcopies:
        copy.start()
    wcopies = []
    for i, (w, wb) in enumerate(((w1, wb1), (w2, wb2))):
        for o in range(2):
            copy = pltpu.make_async_copy(
                w, wb.at[o : o + 3, :, o * channels : (o + 1) * channels], wsem.at[i, o]
            )
            copy.start()
            wcopies.append(copy)
        wb[3, :, 0:channels] = jnp.zeros((wb.shape[1], channels), BF16)
        wb[0, :, channels : 2 * channels] = jnp.zeros((wb.shape[1], channels), BF16)

    amount = (
        has_next.astype(jnp.int32) + has_prev.astype(jnp.int32)
        + has_up.astype(jnp.int32) + has_down.astype(jnp.int32)
    )
    pl.semaphore_wait(barrier, amount)

    def remote(src, dst, sems, k, dev):
        return pltpu.make_async_remote_copy(
            src_ref=src, dst_ref=dst, send_sem=sems[0].at[k], recv_sem=sems[1].at[k],
            device_id=dev, device_id_type=MESH,
        )

    def plan(src, halo, top, bot, sems):
        tail = slice(frames - 2, frames)
        x = [
            remote(src.at[tail, 0], halo.at[:, 0], sems, 0, nxt),
            remote(src.at[tail, last], halo.at[:, last], sems, 1, nxt),
            remote(src.at[tail, 1:last], halo.at[:, 1:last], sems, 2, nxt),
        ]
        forward_up = remote(halo.at[:, 0], bot.at[0:2], sems, 3, up)
        forward_down = remote(halo.at[:, last], top.at[0:2], sems, 4, down)
        late = [
            remote(src.at[tail, 0], bot.at[4:6], sems, 5, up),
            remote(src.at[tail, last], top.at[4:6], sems, 6, down),
        ]
        early = [
            remote(src.at[0:2, 0], bot.at[2:4], sems, 7, up),
            remote(src.at[0:2, last], top.at[2:4], sems, 8, down),
        ]
        return x, (forward_up, forward_down), late, early

    vplan = plan(video, vx, vtop, vbot, (send_v, recv_v))
    splan = plan(mid, sx, stop, sbot, (send_s, recv_s))

    def start_x_edges(p):
        @pl.when(has_next)
        def _():
            for c in p[0][0:2]:
                c.start()

    def start_x_inner(p):
        @pl.when(has_next)
        def _():
            for c in p[0][0:2]:
                c.wait_send()
            p[0][2].start()

    def wait_x_inner(p):
        @pl.when(has_next)
        def _():
            p[0][2].wait_send()

    def start_z(pair):
        @pl.when(has_up)
        def _():
            pair[0].start()

        @pl.when(has_down)
        def _():
            pair[1].start()

    def wait_z(pair):
        @pl.when(has_down)
        def _():
            pair[0].wait_recv()

        @pl.when(has_up)
        def _():
            pair[1].wait_recv()

    def forward(p):
        @pl.when(has_prev)
        def _():
            for c in p[0][0:2]:
                c.wait_recv()
            start_z(p[1])

    def wait_forward(p):
        p[0][2].wait_recv()
        wait_z(p[1])

    def finish_sends(p):
        for pair in (p[2], p[3]):
            @pl.when(has_up)
            def _():
                pair[0].wait_send()

            @pl.when(has_down)
            def _():
                pair[1].wait_send()

        @pl.when(has_prev & has_up)
        def _():
            p[1][0].wait_send()

        @pl.when(has_prev & has_down)
        def _():
            p[1][1].wait_send()

    start_x_edges(vplan)
    start_z(vplan[2])
    start_z(vplan[3])

    for copy in pcopies:
        copy.wait()
    gain1, shift1 = g1[...].reshape(1, channels), s1[...].reshape(1, channels)
    gain2, shift2 = g2[...].reshape(1, channels), s2[...].reshape(1, channels)
    bias1, bias2 = b1[...].reshape(1, channels), b2[...].reshape(1, channels)
    zero_row = jnp.zeros((width, 3 * channels), BF16)

    def first(cells):
        flat = cells.astype(F32).reshape(-1, channels)
        return spread_columns(activate(flat, gain1, shift1), width)

    def plain(cells):
        return spread_columns(cells.astype(F32).reshape(-1, channels), width)

    def edges(x, top, bot, exts, make):
        for cond, halo, row in ((has_up, top, 0), (has_down, bot, rows + 1)):
            @pl.when(cond)
            def _():
                made = make(halo[exts[0] : exts[-1] + 1])
                for k, e in enumerate(exts):
                    x[e, row] = made[k]

            @pl.when(jnp.logical_not(cond))
            def _():
                for e in exts:
                    x[e, row] = zero_row

    def lead(x, p, halo, top, bot, make):
        @pl.when(has_prev)
        def _():
            wait_forward(p)
            for e in range(2):
                x[e, 1 : rows + 1] = make(halo[e])
            edges(x, top, bot, (0, 1), make)

        @pl.when(jnp.logical_not(has_prev))
        def _():
            for e in range(2):
                x[e] = x[2]

    def conv(x, wb, group, pieces, steps):
        combos = [(r, di) for r in steps for di in range(3)]
        depth = 3 * channels
        total = None
        for c in range(0, len(combos), 2):
            cells = jnp.concatenate(
                [
                    jnp.concatenate(
                        [
                            x[2 * group + r, row + di : row + di + count].reshape(count * width, depth)
                            for row, count in pieces
                        ],
                        axis=0,
                    )
                    for r, di in combos[c : c + 2]
                ],
                axis=-1,
            )
            weight = jnp.concatenate(
                [wb[r, di * depth : (di + 1) * depth, :] for r, di in combos[c : c + 2]], axis=0
            )
            product = jnp.dot(cells, weight, preferred_element_type=F32)
            total = product if total is None else total + product
        return total

    def cut(block, pieces):
        start = 0
        for row, count in pieces:
            yield row, count, block[start : start + count]
            start += count

    def finish1(summed, group, pieces):
        for o in range(2):
            part = summed[:, o * channels : (o + 1) * channels] + bias1
            part = activate(part, gain2, shift2)
            frame = 2 * group + o
            narrow = part.astype(BF16).reshape(-1, width, channels)
            for row, count, block in cut(narrow, pieces):
                mid[frame, row : row + count] = block
            for row, count, block in cut(spread_columns(part, width), pieces):
                x2[frame + 2, row + 1 : row + 1 + count] = block

    def finish2(summed, group, pieces):
        for o in range(2):
            part = summed[:, o * channels : (o + 1) * channels] + bias2
            frame = 2 * group + o
            for row, count, block in cut(part.reshape(-1, width, channels), pieces):
                base = vid[frame, row : row + count].astype(F32)
                out[frame, row : row + count] = (base + block).astype(BF16)

    whole = [(0, rows)]
    inner = [(1, rows - 2)]
    outer = [(0, 1), (last, 1)]
    every = range(4)

    vcopy.wait()
    for f in range(frames):
        x1[f + 2, 1 : rows + 1] = first(vid[f])
    start_x_inner(vplan)
    wcopies[0].wait()
    wcopies[1].wait()
    finish1(conv(x1, wb1, 1, inner, every), 1, inner)
    wait_z(vplan[2])
    wait_z(vplan[3])
    forward(vplan)
    edges(x1, vtop, vbot, (2, 3, 4, 5), first)
    finish1(conv(x1, wb1, 1, outer, every), 1, outer)
    start_z(splan[2])
    wait_x_inner(vplan)
    start_x_edges(splan)
    acc[...] = conv(x1, wb1, 0, whole, (2, 3))
    start_x_inner(splan)
    lead(x1, vplan, vx, vtop, vbot, first)
    finish1(acc[...] + conv(x1, wb1, 0, whole, (0, 1)), 0, whole)
    start_z(splan[3])
    forward(splan)
    wcopies[2].wait()
    wcopies[3].wait()
    finish2(conv(x2, wb2, 1, inner, every), 1, inner)
    wait_z(splan[2])
    wait_z(splan[3])
    edges(x2, stop, sbot, (2, 3, 4, 5), plain)
    finish2(conv(x2, wb2, 1, outer, every), 1, outer)
    acc[...] = conv(x2, wb2, 0, whole, (2, 3))
    lead(x2, splan, sx, stop, sbot, plain)
    finish2(acc[...] + conv(x2, wb2, 0, whole, (0, 1)), 0, whole)
    wait_x_inner(splan)
    finish_sends(vplan)
    finish_sends(splan)


def body(video, g1, s1, w1, b1, g2, s2, w2, b2):
    own = video[0]
    in_hbm = functools.partial(pltpu.with_memory_space_constraint, memory_space=pltpu.HBM)
    frames, rows, width, channels = own.shape
    flat = (3, 9 * channels, channels)
    hbm = pl.BlockSpec(memory_space=pltpu.HBM)
    vmem = pl.BlockSpec(memory_space=pltpu.VMEM)
    ext = (frames + 2, rows + 2, width, 3 * channels)
    halo = [
        pltpu.VMEM((2, rows, width, channels), BF16),
        pltpu.VMEM((frames + 2, width, channels), BF16),
        pltpu.VMEM((frames + 2, width, channels), BF16),
    ]
    big = pltpu.VMEM((4, 9 * channels, 2 * channels), BF16)
    own_scratch = pltpu.VMEM(own.shape, BF16)
    dma = pltpu.SemaphoreType.DMA
    result = pl.pallas_call(
        kernel,
        out_shape=pltpu.VMEM(own.shape, BF16),
        in_specs=[hbm] * 9,
        out_specs=vmem,
        scratch_shapes=[
            *[pltpu.VMEM((channels,), F32)] * 6,
            own_scratch,
            pltpu.VMEM(ext, BF16), pltpu.VMEM(ext, BF16),
            big, big,
            own_scratch,
            pltpu.VMEM((rows * width, 2 * channels), F32),
            *halo, *halo,
            dma(()), dma((6,)), dma((2, 2)),
            dma((9,)), dma((9,)), dma((9,)), dma((9,)),
        ],
        compiler_params=pltpu.CompilerParams(
            collective_id=0, has_side_effects=True, vmem_limit_bytes=40 * 2**20
        ),
        cost_estimate=pl.CostEstimate(
            flops=4 * own.size * 27 * channels,
            bytes_accessed=4 * own.size + 8 * w1.size,
            transcendentals=2 * own.size,
        ),
    )(*[in_hbm(a) for a in (own, g1, s1, w1.reshape(flat), b1, g2, s2, w2.reshape(flat), b2)])
    return result[None]


def solution(mesh):
    placed = (P(("grp", "cam"), "ta", "ha", None, None), P(), P(), P(), P(), P(), P(), P(), P())
    return jax.shard_map(
        body,
        mesh=mesh,
        in_specs=placed,
        out_specs=P(("grp", "cam"), "ta", "ha", None, None),
        check_vma=False,
    )
```

```python
import functools

import jax
import jax.numpy as jnp
from jax import lax
from jax.experimental import pallas as pl
from jax.experimental.pallas import tpu as pltpu
from jax.sharding import PartitionSpec as P

MESH = pl.DeviceIdType.MESH
F32 = jnp.float32
BF16 = jnp.bfloat16


def activate(values, gain, shift):
    middle = jnp.mean(values, axis=-1, keepdims=True)
    centred = values - middle
    spread = jnp.mean(centred * centred, axis=-1, keepdims=True)
    normed = centred * lax.rsqrt(spread + 1e-06) * gain + shift
    half = 0.5 * normed
    return half + half * jnp.tanh(half)


def spread_columns(cells, width):
    total, channels = cells.shape
    column = lax.rem(lax.broadcasted_iota(jnp.int32, cells.shape, 0), width)
    left = jnp.where(column == 0, 0.0, pltpu.roll(cells, 1, 0))
    right = jnp.where(column == width - 1, 0.0, pltpu.roll(cells, total - 1, 0))
    wide = jnp.concatenate([left.astype(BF16), cells.astype(BF16), right.astype(BF16)], axis=-1)
    return wide.reshape(total // width, width, 3 * channels)


def kernel(
    video, hg1, hs1, w1, hb1, hg2, hs2, w2, hb2,
    out,
    g1, s1, b1, g2, s2, b2,
    vid, x1, x2, wb1, wb2, mid, acc,
    vx, vtop, vbot, sx, stop, sbot,
    vsem, psem, wsem, send_v, recv_v, send_s, recv_s,
):
    frames, rows, width, channels = video.shape
    last = rows - 1
    ta, tn = lax.axis_index("ta"), lax.axis_size("ta")
    ha, hn = lax.axis_index("ha"), lax.axis_size("ha")
    has_prev, has_next = ta > 0, ta < tn - 1
    has_up, has_down = ha > 0, ha < hn - 1
    nxt, prv = {"ta": lax.rem(ta + 1, tn)}, {"ta": lax.rem(ta + tn - 1, tn)}
    up, down = {"ha": lax.rem(ha + hn - 1, hn)}, {"ha": lax.rem(ha + 1, hn)}

    barrier = pltpu.get_barrier_semaphore()
    for cond, dev in ((has_next, nxt), (has_prev, prv), (has_up, up), (has_down, down)):
        @pl.when(cond)
        def _():
            pl.semaphore_signal(barrier, inc=1, device_id=dev, device_id_type=MESH)

    vcopy = pltpu.make_async_copy(video, vid, vsem)
    vcopy.start()
    params = ((hg1, g1), (hs1, s1), (hb1, b1), (hg2, g2), (hs2, s2), (hb2, b2))
    pcopies = [pltpu.make_async_copy(h, v, psem.at[i]) for i, (h, v) in enumerate(params)]
    for copy in pcopies:
        copy.start()
    wcopies = []
    for i, (w, wb) in enumerate(((w1, wb1), (w2, wb2))):
        for o in range(2):
            copy = pltpu.make_async_copy(
                w, wb.at[o : o + 3, :, o * channels : (o + 1) * channels], wsem.at[i, o]
            )
            copy.start()
            wcopies.append(copy)
        wb[3, :, 0:channels] = jnp.zeros((wb.shape[1], channels), BF16)
        wb[0, :, channels : 2 * channels] = jnp.zeros((wb.shape[1], channels), BF16)

    amount = (
        has_next.astype(jnp.int32) + has_prev.astype(jnp.int32)
        + has_up.astype(jnp.int32) + has_down.astype(jnp.int32)
    )
    pl.semaphore_wait(barrier, amount)

    def remote(src, dst, sems, k, dev):
        return pltpu.make_async_remote_copy(
            src_ref=src, dst_ref=dst, send_sem=sems[0].at[k], recv_sem=sems[1].at[k],
            device_id=dev, device_id_type=MESH,
        )

    def plan(src, halo, top, bot, sems):
        tail = slice(frames - 2, frames)
        x = [
            remote(src.at[tail, 0], halo.at[:, 0], sems, 0, nxt),
            remote(src.at[tail, last], halo.at[:, last], sems, 1, nxt),
            remote(src.at[tail, 1:last], halo.at[:, 1:last], sems, 2, nxt),
        ]
        forward_up = remote(halo.at[:, 0], bot.at[0:2], sems, 3, up)
        forward_down = remote(halo.at[:, last], top.at[0:2], sems, 4, down)
        late = [
            remote(src.at[tail, 0], bot.at[4:6], sems, 5, up),
            remote(src.at[tail, last], top.at[4:6], sems, 6, down),
        ]
        early = [
            remote(src.at[0:2, 0], bot.at[2:4], sems, 7, up),
            remote(src.at[0:2, last], top.at[2:4], sems, 8, down),
        ]
        return x, (forward_up, forward_down), late, early

    vplan = plan(video, vx, vtop, vbot, (send_v, recv_v))
    splan = plan(mid, sx, stop, sbot, (send_s, recv_s))

    def start_x_edges(p):
        @pl.when(has_next)
        def _():
            for c in p[0][0:2]:
                c.start()

    def start_x_inner(p):
        @pl.when(has_next)
        def _():
            for c in p[0][0:2]:
                c.wait_send()
            p[0][2].start()

    def wait_x_inner(p):
        @pl.when(has_next)
        def _():
            p[0][2].wait_send()

    def start_z(pair):
        @pl.when(has_up)
        def _():
            pair[0].start()

        @pl.when(has_down)
        def _():
            pair[1].start()

    def wait_z(pair):
        @pl.when(has_down)
        def _():
            pair[0].wait_recv()

        @pl.when(has_up)
        def _():
            pair[1].wait_recv()

    def forward(p):
        @pl.when(has_prev)
        def _():
            for c in p[0][0:2]:
                c.wait_recv()
            start_z(p[1])

    def wait_forward(p):
        p[0][2].wait_recv()
        wait_z(p[1])

    def finish_sends(p):
        for pair in (p[2], p[3]):
            @pl.when(has_up)
            def _():
                pair[0].wait_send()

            @pl.when(has_down)
            def _():
                pair[1].wait_send()

        @pl.when(has_prev & has_up)
        def _():
            p[1][0].wait_send()

        @pl.when(has_prev & has_down)
        def _():
            p[1][1].wait_send()

    start_x_edges(vplan)
    start_z(vplan[2])
    start_z(vplan[3])

    for copy in pcopies:
        copy.wait()
    gain1, shift1 = g1[...].reshape(1, channels), s1[...].reshape(1, channels)
    gain2, shift2 = g2[...].reshape(1, channels), s2[...].reshape(1, channels)
    bias1, bias2 = b1[...].reshape(1, channels), b2[...].reshape(1, channels)
    zero_row = jnp.zeros((width, 3 * channels), BF16)

    def first(cells):
        flat = cells.astype(F32).reshape(-1, channels)
        return spread_columns(activate(flat, gain1, shift1), width)

    def plain(cells):
        return spread_columns(cells.astype(F32).reshape(-1, channels), width)

    def edges(x, top, bot, exts, make):
        for cond, halo, row in ((has_up, top, 0), (has_down, bot, rows + 1)):
            @pl.when(cond)
            def _():
                made = make(halo[exts[0] : exts[-1] + 1])
                for k, e in enumerate(exts):
                    x[e, row] = made[k]

            @pl.when(jnp.logical_not(cond))
            def _():
                for e in exts:
                    x[e, row] = zero_row

    def lead(x, p, halo, top, bot, make):
        @pl.when(has_prev)
        def _():
            wait_forward(p)
            for e in range(2):
                x[e, 1 : rows + 1] = make(halo[e])
            edges(x, top, bot, (0, 1), make)

        @pl.when(jnp.logical_not(has_prev))
        def _():
            for e in range(2):
                x[e] = x[2]

    def conv(x, wb, group, pieces, steps):
        combos = [(r, di) for r in steps for di in range(3)]
        depth = 3 * channels
        total = None
        for c in range(0, len(combos), 2):
            cells = jnp.concatenate(
                [
                    jnp.concatenate(
                        [
                            x[2 * group + r, row + di : row + di + count].reshape(count * width, depth)
                            for row, count in pieces
                        ],
                        axis=0,
                    )
                    for r, di in combos[c : c + 2]
                ],
                axis=-1,
            )
            weight = jnp.concatenate(
                [wb[r, di * depth : (di + 1) * depth, :] for r, di in combos[c : c + 2]], axis=0
            )
            product = jnp.dot(cells, weight, preferred_element_type=F32)
            total = product if total is None else total + product
        return total

    def cut(block, pieces):
        start = 0
        for row, count in pieces:
            yield row, count, block[start : start + count]
            start += count

    def finish1(summed, group, pieces):
        for o in range(2):
            part = summed[:, o * channels : (o + 1) * channels] + bias1
            part = activate(part, gain2, shift2)
            frame = 2 * group + o
            narrow = part.astype(BF16).reshape(-1, width, channels)
            for row, count, block in cut(narrow, pieces):
                mid[frame, row : row + count] = block
            for row, count, block in cut(spread_columns(part, width), pieces):
                x2[frame + 2, row + 1 : row + 1 + count] = block

    def finish2(summed, group, pieces):
        for o in range(2):
            part = summed[:, o * channels : (o + 1) * channels] + bias2
            frame = 2 * group + o
            for row, count, block in cut(part.reshape(-1, width, channels), pieces):
                base = vid[frame, row : row + count].astype(F32)
                out[frame, row : row + count] = (base + block).astype(BF16)

    whole = [(0, rows)]
    inner = [(1, rows - 2)]
    outer = [(0, 1), (last, 1)]
    every = range(4)

    vcopy.wait()
    for f in range(frames):
        x1[f + 2, 1 : rows + 1] = first(vid[f])
    start_x_inner(vplan)
    wcopies[0].wait()
    wcopies[1].wait()
    finish1(conv(x1, wb1, 1, inner, every), 1, inner)
    wait_z(vplan[2])
    wait_z(vplan[3])
    forward(vplan)
    edges(x1, vtop, vbot, (2, 3, 4, 5), first)
    finish1(conv(x1, wb1, 1, outer, every), 1, outer)
    start_z(splan[2])
    acc[...] = conv(x1, wb1, 0, whole, (2, 3))
    wait_x_inner(vplan)
    start_x_edges(splan)
    lead(x1, vplan, vx, vtop, vbot, first)
    finish1(acc[...] + conv(x1, wb1, 0, whole, (0, 1)), 0, whole)
    start_z(splan[3])
    start_x_inner(splan)
    forward(splan)
    wcopies[2].wait()
    wcopies[3].wait()
    finish2(conv(x2, wb2, 1, inner, every), 1, inner)
    wait_z(splan[2])
    wait_z(splan[3])
    edges(x2, stop, sbot, (2, 3, 4, 5), plain)
    finish2(conv(x2, wb2, 1, outer, every), 1, outer)
    acc[...] = conv(x2, wb2, 0, whole, (2, 3))
    lead(x2, splan, sx, stop, sbot, plain)
    finish2(acc[...] + conv(x2, wb2, 0, whole, (0, 1)), 0, whole)
    wait_x_inner(splan)
    finish_sends(vplan)
    finish_sends(splan)


def body(video, g1, s1, w1, b1, g2, s2, w2, b2):
    own = video[0]
    in_hbm = functools.partial(pltpu.with_memory_space_constraint, memory_space=pltpu.HBM)
    frames, rows, width, channels = own.shape
    flat = (3, 9 * channels, channels)
    hbm = pl.BlockSpec(memory_space=pltpu.HBM)
    vmem = pl.BlockSpec(memory_space=pltpu.VMEM)
    ext = (frames + 2, rows + 2, width, 3 * channels)
    halo = [
        pltpu.VMEM((2, rows, width, channels), BF16),
        pltpu.VMEM((frames + 2, width, channels), BF16),
        pltpu.VMEM((frames + 2, width, channels), BF16),
    ]
    big = pltpu.VMEM((4, 9 * channels, 2 * channels), BF16)
    own_scratch = pltpu.VMEM(own.shape, BF16)
    dma = pltpu.SemaphoreType.DMA
    result = pl.pallas_call(
        kernel,
        out_shape=pltpu.VMEM(own.shape, BF16),
        in_specs=[hbm] * 9,
        out_specs=vmem,
        scratch_shapes=[
            *[pltpu.VMEM((channels,), F32)] * 6,
            own_scratch,
            pltpu.VMEM(ext, BF16), pltpu.VMEM(ext, BF16),
            big, big,
            own_scratch,
            pltpu.VMEM((rows * width, 2 * channels), F32),
            *halo, *halo,
            dma(()), dma((6,)), dma((2, 2)),
            dma((9,)), dma((9,)), dma((9,)), dma((9,)),
        ],
        compiler_params=pltpu.CompilerParams(
            collective_id=0, has_side_effects=True, vmem_limit_bytes=40 * 2**20
        ),
        cost_estimate=pl.CostEstimate(
            flops=4 * own.size * 27 * channels,
            bytes_accessed=4 * own.size + 8 * w1.size,
            transcendentals=2 * own.size,
        ),
    )(*[in_hbm(a) for a in (own, g1, s1, w1.reshape(flat), b1, g2, s2, w2.reshape(flat), b2)])
    return result[None]


def solution(mesh):
    placed = (P(("grp", "cam"), "ta", "ha", None, None), P(), P(), P(), P(), P(), P(), P(), P())
    return jax.shard_map(
        body,
        mesh=mesh,
        in_specs=placed,
        out_specs=P(("grp", "cam"), "ta", "ha", None, None),
        check_vma=False,
    )
```

```python
import functools

import jax
import jax.numpy as jnp
from jax import lax
from jax.experimental import pallas as pl
from jax.experimental.pallas import tpu as pltpu
from jax.sharding import PartitionSpec as P

MESH = pl.DeviceIdType.MESH
F32 = jnp.float32
BF16 = jnp.bfloat16


def activate(values, gain, shift):
    middle = jnp.mean(values, axis=-1, keepdims=True)
    centred = values - middle
    spread = jnp.mean(centred * centred, axis=-1, keepdims=True)
    normed = centred * lax.rsqrt(spread + 1e-06) * gain + shift
    half = 0.5 * normed
    return half + half * jnp.tanh(half)


def spread_columns(cells, width):
    total, channels = cells.shape
    column = lax.rem(lax.broadcasted_iota(jnp.int32, cells.shape, 0), width)
    left = jnp.where(column == 0, 0.0, pltpu.roll(cells, 1, 0))
    right = jnp.where(column == width - 1, 0.0, pltpu.roll(cells, total - 1, 0))
    wide = jnp.concatenate([left.astype(BF16), cells.astype(BF16), right.astype(BF16)], axis=-1)
    return wide.reshape(total // width, width, 3 * channels)


def kernel(
    video, hg1, hs1, w1, hb1, hg2, hs2, w2, hb2,
    out,
    g1, s1, b1, g2, s2, b2,
    vid, x1, x2, wb1, wb2, mid, acc,
    vx, vtop, vbot, sx, stop, sbot,
    vsem, psem, wsem, send_v, recv_v, send_s, recv_s,
):
    frames, rows, width, channels = video.shape
    last = rows - 1
    ta, tn = lax.axis_index("ta"), lax.axis_size("ta")
    ha, hn = lax.axis_index("ha"), lax.axis_size("ha")
    has_prev, has_next = ta > 0, ta < tn - 1
    has_up, has_down = ha > 0, ha < hn - 1
    nxt, prv = {"ta": lax.rem(ta + 1, tn)}, {"ta": lax.rem(ta + tn - 1, tn)}
    up, down = {"ha": lax.rem(ha + hn - 1, hn)}, {"ha": lax.rem(ha + 1, hn)}

    barrier = pltpu.get_barrier_semaphore()
    for cond, dev in ((has_next, nxt), (has_prev, prv), (has_up, up), (has_down, down)):
        @pl.when(cond)
        def _():
            pl.semaphore_signal(barrier, inc=1, device_id=dev, device_id_type=MESH)

    vcopy = pltpu.make_async_copy(video, vid, vsem)
    vcopy.start()
    params = ((hg1, g1), (hs1, s1), (hb1, b1), (hg2, g2), (hs2, s2), (hb2, b2))
    pcopies = [pltpu.make_async_copy(h, v, psem.at[i]) for i, (h, v) in enumerate(params)]
    for copy in pcopies:
        copy.start()
    wcopies = []
    for i, (w, wb) in enumerate(((w1, wb1), (w2, wb2))):
        for o in range(2):
            copy = pltpu.make_async_copy(
                w, wb.at[o : o + 3, :, o * channels : (o + 1) * channels], wsem.at[i, o]
            )
            copy.start()
            wcopies.append(copy)
        wb[3, :, 0:channels] = jnp.zeros((wb.shape[1], channels), BF16)
        wb[0, :, channels : 2 * channels] = jnp.zeros((wb.shape[1], channels), BF16)

    amount = (
        has_next.astype(jnp.int32) + has_prev.astype(jnp.int32)
        + has_up.astype(jnp.int32) + has_down.astype(jnp.int32)
    )
    pl.semaphore_wait(barrier, amount)

    def remote(src, dst, sems, k, dev):
        return pltpu.make_async_remote_copy(
            src_ref=src, dst_ref=dst, send_sem=sems[0].at[k], recv_sem=sems[1].at[k],
            device_id=dev, device_id_type=MESH,
        )

    def plan(src, halo, top, bot, sems):
        tail = slice(frames - 2, frames)
        x = [
            remote(src.at[tail, 0], halo.at[:, 0], sems, 0, nxt),
            remote(src.at[tail, last], halo.at[:, last], sems, 1, nxt),
            remote(src.at[tail, 1:last], halo.at[:, 1:last], sems, 2, nxt),
        ]
        forward_up = remote(halo.at[:, 0], bot.at[0:2], sems, 3, up)
        forward_down = remote(halo.at[:, last], top.at[0:2], sems, 4, down)
        late = [
            remote(src.at[tail, 0], bot.at[4:6], sems, 5, up),
            remote(src.at[tail, last], top.at[4:6], sems, 6, down),
        ]
        early = [
            remote(src.at[0:2, 0], bot.at[2:4], sems, 7, up),
            remote(src.at[0:2, last], top.at[2:4], sems, 8, down),
        ]
        return x, (forward_up, forward_down), late, early

    vplan = plan(video, vx, vtop, vbot, (send_v, recv_v))
    splan = plan(mid, sx, stop, sbot, (send_s, recv_s))

    def start_x_edges(p):
        @pl.when(has_next)
        def _():
            for c in p[0][0:2]:
                c.start()

    def start_x_inner(p):
        @pl.when(has_next)
        def _():
            for c in p[0][0:2]:
                c.wait_send()
            p[0][2].start()

    def wait_x_inner(p):
        @pl.when(has_next)
        def _():
            p[0][2].wait_send()

    def start_z(pair):
        @pl.when(has_up)
        def _():
            pair[0].start()

        @pl.when(has_down)
        def _():
            pair[1].start()

    def wait_z(pair):
        @pl.when(has_down)
        def _():
            pair[0].wait_recv()

        @pl.when(has_up)
        def _():
            pair[1].wait_recv()

    def forward(p):
        @pl.when(has_prev)
        def _():
            for c in p[0][0:2]:
                c.wait_recv()
            start_z(p[1])

    def finish_sends(p):
        for pair in (p[2], p[3]):
            @pl.when(has_up)
            def _():
                pair[0].wait_send()

            @pl.when(has_down)
            def _():
                pair[1].wait_send()

        @pl.when(has_prev & has_up)
        def _():
            p[1][0].wait_send()

        @pl.when(has_prev & has_down)
        def _():
            p[1][1].wait_send()

    start_x_edges(vplan)
    start_z(vplan[2])
    start_z(vplan[3])

    for copy in pcopies:
        copy.wait()
    gain1, shift1 = g1[...].reshape(1, channels), s1[...].reshape(1, channels)
    gain2, shift2 = g2[...].reshape(1, channels), s2[...].reshape(1, channels)
    bias1, bias2 = b1[...].reshape(1, channels), b2[...].reshape(1, channels)
    zero_row = jnp.zeros((width, 3 * channels), BF16)

    def first(cells):
        flat = cells.astype(F32).reshape(-1, channels)
        return spread_columns(activate(flat, gain1, shift1), width)

    def plain(cells):
        return spread_columns(cells.astype(F32).reshape(-1, channels), width)

    def edges(x, top, bot, exts, make):
        for cond, halo, row in ((has_up, top, 0), (has_down, bot, rows + 1)):
            @pl.when(cond)
            def _():
                made = make(halo[exts[0] : exts[-1] + 1])
                for k, e in enumerate(exts):
                    x[e, row] = made[k]

            @pl.when(jnp.logical_not(cond))
            def _():
                for e in exts:
                    x[e, row] = zero_row

    def lead(x, p, halo, top, bot, make):
        @pl.when(has_prev)
        def _():
            wait_z(p[1])
            for row in (0, last):
                made = make(halo[:, row])
                for e in range(2):
                    x[e, row + 1] = made[e]
            edges(x, top, bot, (0, 1), make)
            p[0][2].wait_recv()
            for e in range(2):
                x[e, 2:rows] = make(halo[e, 1:last])

        @pl.when(jnp.logical_not(has_prev))
        def _():
            for e in range(2):
                x[e] = x[2]

    def conv(x, wb, group, pieces, steps):
        combos = [(r, di) for r in steps for di in range(3)]
        depth = 3 * channels
        total = None
        for c in range(0, len(combos), 2):
            cells = jnp.concatenate(
                [
                    jnp.concatenate(
                        [
                            x[2 * group + r, row + di : row + di + count].reshape(count * width, depth)
                            for row, count in pieces
                        ],
                        axis=0,
                    )
                    for r, di in combos[c : c + 2]
                ],
                axis=-1,
            )
            weight = jnp.concatenate(
                [wb[r, di * depth : (di + 1) * depth, :] for r, di in combos[c : c + 2]], axis=0
            )
            product = jnp.dot(cells, weight, preferred_element_type=F32)
            total = product if total is None else total + product
        return total

    def cut(block, pieces):
        start = 0
        for row, count in pieces:
            yield row, count, block[start : start + count]
            start += count

    def finish1(summed, group, pieces, between=None):
        for o in range(2):
            if o == 1 and between is not None:
                between()
            part = summed[:, o * channels : (o + 1) * channels] + bias1
            part = activate(part, gain2, shift2)
            frame = 2 * group + o
            narrow = part.astype(BF16).reshape(-1, width, channels)
            for row, count, block in cut(narrow, pieces):
                mid[frame, row : row + count] = block
            for row, count, block in cut(spread_columns(part, width), pieces):
                x2[frame + 2, row + 1 : row + 1 + count] = block

    def finish2(summed, group, pieces):
        for o in range(2):
            part = summed[:, o * channels : (o + 1) * channels] + bias2
            frame = 2 * group + o
            for row, count, block in cut(part.reshape(-1, width, channels), pieces):
                base = vid[frame, row : row + count].astype(F32)
                out[frame, row : row + count] = (base + block).astype(BF16)

    whole = [(0, rows)]
    inner = [(1, rows - 2)]
    outer = [(0, 1), (last, 1)]
    every = range(4)

    vcopy.wait()
    for f in range(frames):
        x1[f + 2, 1 : rows + 1] = first(vid[f])
    start_x_inner(vplan)
    wcopies[0].wait()
    wcopies[1].wait()
    finish1(conv(x1, wb1, 1, inner, every), 1, inner)
    wait_z(vplan[2])
    wait_z(vplan[3])
    forward(vplan)
    edges(x1, vtop, vbot, (2, 3, 4, 5), first)
    finish1(conv(x1, wb1, 1, outer, every), 1, outer)
    start_z(splan[2])
    acc[...] = conv(x1, wb1, 0, whole, (2, 3))
    wait_x_inner(vplan)
    start_x_edges(splan)
    lead(x1, vplan, vx, vtop, vbot, first)
    finish1(acc[...] + conv(x1, wb1, 0, whole, (0, 1)), 0, whole, lambda: start_x_inner(splan))
    start_z(splan[3])
    forward(splan)
    wcopies[2].wait()
    wcopies[3].wait()
    finish2(conv(x2, wb2, 1, inner, every), 1, inner)
    wait_z(splan[2])
    wait_z(splan[3])
    edges(x2, stop, sbot, (2, 3, 4, 5), plain)
    finish2(conv(x2, wb2, 1, outer, every), 1, outer)
    acc[...] = conv(x2, wb2, 0, whole, (2, 3))
    lead(x2, splan, sx, stop, sbot, plain)
    finish2(acc[...] + conv(x2, wb2, 0, whole, (0, 1)), 0, whole)
    wait_x_inner(splan)
    finish_sends(vplan)
    finish_sends(splan)


def body(video, g1, s1, w1, b1, g2, s2, w2, b2):
    own = video[0]
    in_hbm = functools.partial(pltpu.with_memory_space_constraint, memory_space=pltpu.HBM)
    frames, rows, width, channels = own.shape
    flat = (3, 9 * channels, channels)
    hbm = pl.BlockSpec(memory_space=pltpu.HBM)
    vmem = pl.BlockSpec(memory_space=pltpu.VMEM)
    ext = (frames + 2, rows + 2, width, 3 * channels)
    halo = [
        pltpu.VMEM((2, rows, width, channels), BF16),
        pltpu.VMEM((frames + 2, width, channels), BF16),
        pltpu.VMEM((frames + 2, width, channels), BF16),
    ]
    big = pltpu.VMEM((4, 9 * channels, 2 * channels), BF16)
    own_scratch = pltpu.VMEM(own.shape, BF16)
    dma = pltpu.SemaphoreType.DMA
    result = pl.pallas_call(
        kernel,
        out_shape=pltpu.VMEM(own.shape, BF16),
        in_specs=[hbm] * 9,
        out_specs=vmem,
        scratch_shapes=[
            *[pltpu.VMEM((channels,), F32)] * 6,
            own_scratch,
            pltpu.VMEM(ext, BF16), pltpu.VMEM(ext, BF16),
            big, big,
            own_scratch,
            pltpu.VMEM((rows * width, 2 * channels), F32),
            *halo, *halo,
            dma(()), dma((6,)), dma((2, 2)),
            dma((9,)), dma((9,)), dma((9,)), dma((9,)),
        ],
        compiler_params=pltpu.CompilerParams(
            collective_id=0, has_side_effects=True, vmem_limit_bytes=40 * 2**20
        ),
        cost_estimate=pl.CostEstimate(
            flops=4 * own.size * 27 * channels,
            bytes_accessed=4 * own.size + 8 * w1.size,
            transcendentals=2 * own.size,
        ),
    )(*[in_hbm(a) for a in (own, g1, s1, w1.reshape(flat), b1, g2, s2, w2.reshape(flat), b2)])
    return result[None]


def solution(mesh):
    placed = (P(("grp", "cam"), "ta", "ha", None, None), P(), P(), P(), P(), P(), P(), P(), P())
    return jax.shard_map(
        body,
        mesh=mesh,
        in_specs=placed,
        out_specs=P(("grp", "cam"), "ta", "ha", None, None),
        check_vma=False,
    )
```
